32 devices in a mesh: groups: 2 (over y), cache: 4 (over z), mp: 2 (over x), sub: 2 (over core).
Axes of the slice: x: 2, y: 2, z: 4, core: 2. Of those that a mesh axis runs over, the one named last changes fastest.
Arguments:
- conv_input: bfloat16 [8, 256, 20480], P(('groups', 'cache'), None, ('mp', 'sub')), parts along dimension 0, may hold values from -6 to 6
- dt_raw: float32 [8, 256, 256], P(('groups', 'cache'), None, ('mp', 'sub')), parts along dimension 0
- conv_weight: float32 [4, 20480], P(None, ('mp', 'sub')), may hold values from -3 to 3
- conv_bias: float32 [20480], P(('mp', 'sub')), may hold values from -3 to 3
- dt_bias: float32 [256], P(('mp', 'sub')), may hold values from -4.5 to -1.5
- a_log: float32 [256], P(('mp', 'sub')), may hold values from -4.5 to 0.5
- d_skip: float32 [256], P(('mp', 'sub')), may hold values from 0.5 to 1.5
- cache_state: bfloat16 [8, 256, 64, 256], P(('groups', 'cache'), ('mp', 'sub')), parts along dimension 0, may hold values from -2 to 2
- cache_tail: bfloat16 [8, 3, 20480], P(('groups', 'cache'), None, ('mp', 'sub')), parts along dimension 0, may hold values from -6 to 6
- hit_slot: int32 [8], P(('groups', 'cache')), parts along dimension 0, may hold values from 0 to 3, as said below
- hit_mask: int32 [8], P(('groups', 'cache')), parts along dimension 0, may hold values 0 or 1
- suffix_len: int32 [8], P(('groups', 'cache')), parts along dimension 0, may hold values from 32 to 256
- write_slot: int32 [8], P(('groups', 'cache')), parts along dimension 0, may hold values from 0 to 3, as said below
Outputs:
- y_out: bfloat16 [8, 256, 16384], P(('groups', 'cache'), None, ('mp', 'sub')), parts along dimension 0
- new_state: bfloat16 [8, 256, 64, 256], P(('groups', 'cache'), ('mp', 'sub')), parts along dimension 0
- new_tail: bfloat16 [8, 3, 20480], P(('groups', 'cache'), None, ('mp', 'sub')), parts along dimension 0
The draws below stay inside these ranges and needn't reach their ends.
There are 2 independent parts, one for each index of `groups`. The reference program is written for one: setup_inputs(seed, part) draws one part's arguments, and reference() takes and returns one part's arrays. A program takes and returns all parts, laid end to end along the dimension named above; an argument that names none is the same for every part. Nothing has to cross between parts.
Inputs may be any that keep to these rules, and one draw needn't show every extreme that they name: `hit_slot`: owner of slot s is index s // 1 of cache; about half of the requests share one drawn slot. `write_slot`: each slot once; slot w belongs to index w // 1 of cache.
All inputs are finite; a program needn't handle non-finite values. No bound on the sum of `hit_mask` on one device may be relied on, other than what follows from the above.
Results may differ from the reference program's by a relative error of at most 0.001.
Values may be sent and summed in bfloat16 or wider, within the bound.
A program may use at most 128 MiB of HBM per device.

```python
import jax
import jax.numpy as jnp
from jax import lax

HEADS = 256
HEAD_P = 64
NSTATE = 256
GROUPS = 8
CONV_W = 4
SPAN = 256
SUFFIX_POSITIONS = 256
CONV_ALL = 20480
REQUEST_COUNT = 4
CACHE_SLOTS = 4


def draw_dt_raw(key, part):
    key = jax.random.fold_in(key, 23)
    key_base_random, key_clustered = jax.random.split(key)
    base_sample = 0.6 * jax.random.normal(key_base_random, (REQUEST_COUNT, SUFFIX_POSITIONS, HEADS), jnp.float32)
    clustered_hits = (jax.random.randint(key_clustered, (REQUEST_COUNT, SUFFIX_POSITIONS, 1), 0, SUFFIX_POSITIONS) < 3).astype(jnp.float32)
    return base_sample + 5.0 * clustered_hits


def draw_hit_slot(key, part):
    key = jax.random.fold_in(key, 11)
    key_base_random, key_hot, key_pick, key_order = jax.random.split(key, 4)
    base_slots = jax.random.randint(key_base_random, (REQUEST_COUNT,), 0, CACHE_SLOTS)
    hot_slot = jax.random.randint(key_hot, (), 0, CACHE_SLOTS)
    picked = jax.random.randint(key_pick, (REQUEST_COUNT,), 0, 2)
    slots_all = jnp.where(picked > 0, hot_slot, base_slots)
    order_all = jax.random.permutation(key_order, REQUEST_COUNT)
    slots_all = slots_all.at[order_all[0]].set(0).at[order_all[1]].set(CACHE_SLOTS - 1)
    return slots_all.astype(jnp.int32)


def draw_suffix_len(key, part):
    key = jax.random.fold_in(key, 37)
    key_len, key_order = jax.random.split(key)
    lengths_all = jax.random.randint(key_len, (REQUEST_COUNT,), SUFFIX_POSITIONS // 8, SUFFIX_POSITIONS + 1)
    order_all = jax.random.permutation(key_order, REQUEST_COUNT)
    lengths_all = lengths_all.at[order_all[0]].set(SUFFIX_POSITIONS).at[order_all[1]].set(SUFFIX_POSITIONS // 8)
    return lengths_all.astype(jnp.int32)


def draw_write_slot(key, part):
    key = jax.random.fold_in(key, 53)
    order_all = jax.random.permutation(key, REQUEST_COUNT)
    return order_all.astype(jnp.int32)


def set_ends(array, rng, least, top_value):
    spot = [jax.random.randint(jax.random.fold_in(rng, axis), (), 0, length) for axis, length in enumerate(array.shape)]
    longest = array.shape.index(max(array.shape))
    next_to = spot[:longest] + [(spot[longest] + 1) % array.shape[longest]] + spot[longest + 1:]
    return array.at[tuple(spot)].set(least).at[tuple(next_to)].set(top_value)


def steps_of(stream_key, shape, shards, smallest, top_value):
    factor_of = 1.0
    for dim, blocks in shards:
        draws = jax.random.uniform(jax.random.fold_in(jax.random.fold_in(stream_key, 6), dim), (blocks,), jnp.float32, smallest / len(shards), top_value / len(shards))
        factor_of = factor_of * jnp.repeat(jnp.exp(draws), shape[dim] // blocks).reshape((-1,) + (1,) * (len(shape) - 1 - dim))
    return factor_of


def noise(key, shape, deviation, reach, cuts=(), held_as=jnp.bfloat16):
    result = jax.random.normal(key, shape, jnp.float32) * deviation
    if len(cuts) > 0:
        result = steps_of(key, shape, cuts, -0.22, 0.18) * result
    return jnp.clip(result, min=-reach, max=reach).astype(held_as)


def setup_inputs(seed: int = 0, part: int = 0) -> dict:
    splits = jax.random.split(jax.random.key(seed), 14)
    part_splits = jax.random.split(jax.random.fold_in(splits[13], part), 14)
    return {
        "conv_input": noise(part_splits[0], (REQUEST_COUNT, SUFFIX_POSITIONS, CONV_ALL), 1.0, 6.0, ((0, 4), (2, 4))),
        "dt_raw": draw_dt_raw(jax.random.fold_in(jax.random.fold_in(splits[13], part), 71), part),
        "conv_weight": noise(splits[2], (CONV_W, CONV_ALL), CONV_W ** -0.5, 3.0, ((1, 4),), jnp.float32),
        "conv_bias": noise(splits[3], (CONV_ALL,), 0.5, 3.0, ((0, 4),), jnp.float32),
        "dt_bias": jnp.clip(-4.5 + 3.0 * jax.random.uniform(splits[4], (HEADS,), jnp.float32) ** steps_of(splits[4], (HEADS,), ((0, 4),), -0.2, 0.2), -4.5, -1.5),
        "a_log": jnp.clip(-4.5 + 5.0 * jax.random.uniform(splits[5], (HEADS,), jnp.float32) ** steps_of(splits[5], (HEADS,), ((0, 4),), -0.2, 0.2), -4.5, 0.5),
        "d_skip": jnp.clip(0.5 + 1.0 * jax.random.uniform(splits[6], (HEADS,), jnp.float32) ** steps_of(splits[6], (HEADS,), ((0, 4),), -0.2, 0.2), 0.5, 1.5),
        "cache_state": noise(part_splits[7], (CACHE_SLOTS, HEADS, HEAD_P, NSTATE), 0.3, 2.0, ((0, 4), (1, 4))),
        "cache_tail": noise(part_splits[8], (CACHE_SLOTS, CONV_W - 1, CONV_ALL), 1.0, 6.0, ((0, 4), (2, 4))),
        "hit_slot": draw_hit_slot(jax.random.fold_in(jax.random.fold_in(splits[13], part), 71), part),
        "hit_mask": set_ends((jax.random.randint(part_splits[10], (REQUEST_COUNT,), 0, 4) < 3).astype(jnp.int32), jax.random.fold_in(part_splits[10], 1), 0, 1),
        "suffix_len": draw_suffix_len(jax.random.fold_in(jax.random.fold_in(splits[13], part), 71), part),
        "write_slot": draw_write_slot(jax.random.fold_in(jax.random.fold_in(splits[13], part), 71), part),
    }


highest = lax.Precision.HIGHEST


def conv_and_scan(conv_input, dt_raw, prev_state, prev_tail, length, conv_weight, conv_bias, dt_bias, a_log, d_skip):
    steps_total = conv_input.shape[0]
    conv_width = conv_weight.shape[0]
    head_count = dt_raw.shape[1]
    per_group = HEADS // GROUPS
    groups_here = head_count // per_group
    x_width = per_group * HEAD_P
    extended = jnp.concatenate([prev_tail, conv_input.astype(jnp.float32)], axis=0)
    conv_sum = conv_bias[None, :] + conv_weight[0][None, :] * extended[0:steps_total]
    for shift_k in range(1, conv_width):
        conv_sum = conv_sum + conv_weight[shift_k][None, :] * extended[shift_k:shift_k + steps_total]
    activated = jax.nn.silu(conv_sum).reshape(steps_total, groups_here, x_width + 2 * NSTATE)
    x_heads = activated[:, :, :x_width].reshape(steps_total, groups_here, per_group, HEAD_P)
    b_group = activated[:, :, x_width:x_width + NSTATE]
    output_coeff_group = activated[:, :, x_width + NSTATE:]
    tail_rows = lax.dynamic_slice_in_dim(extended, length.astype(jnp.int32), conv_width - 1, 0)
    position = jnp.arange(steps_total, dtype=jnp.int32)
    live_mask = (position < length).astype(jnp.float32)
    step_size = jax.nn.softplus(dt_raw + dt_bias[None, :]) * live_mask[:, None]
    log_decay = (step_size * (-jnp.exp(a_log))[None, :]).reshape(steps_total, groups_here, per_group)
    x_scaled = x_heads * step_size.reshape(steps_total, groups_here, per_group)[..., None]
    carry_state = prev_state.reshape(groups_here, per_group, HEAD_P, NSTATE)
    tri_mask = jnp.tril(jnp.ones((SPAN, SPAN), dtype=bool))
    pieces_out = []
    for offset in range(0, steps_total, SPAN):
        cum_decay = jnp.cumsum(log_decay[offset:offset + SPAN], axis=0)
        gap_grid = jnp.where(tri_mask[:, :, None, None], cum_decay[:, None] - cum_decay[None, :], -jnp.inf)
        decay_grid = jnp.exp(gap_grid)
        c_block = output_coeff_group[offset:offset + SPAN]
        b_block = b_group[offset:offset + SPAN]
        x_block = x_scaled[offset:offset + SPAN]
        intersection = jnp.einsum('ign,jgn->ijg', c_block, b_block, precision=highest)
        weighted = decay_grid * intersection[..., None]
        inner_part = jnp.einsum('ijgk,jgkp->igkp', weighted, x_block, precision=highest)
        carried_over = jnp.einsum('ign,gkpn->igkp', c_block, carry_state, precision=highest) * jnp.exp(cum_decay)[..., None]
        tail_decay = jnp.exp(cum_decay[-1][None] - cum_decay)
        x_tail = x_block * tail_decay[..., None]
        state_add = jnp.einsum('jgkp,jgn->gkpn', x_tail, b_block, precision=highest)
        carry_state = jnp.exp(cum_decay[-1])[..., None, None] * carry_state + state_add
        pieces_out.append(inner_part + carried_over)
    y_heads = jnp.concatenate(pieces_out, axis=0) + d_skip.reshape(groups_here, per_group)[None, :, :, None] * x_heads
    y_heads = y_heads * live_mask[:, None, None, None]
    return (y_heads.reshape(steps_total, head_count * HEAD_P), carry_state.reshape(head_count, HEAD_P, NSTATE), tail_rows, output_coeff_group, log_decay, live_mask)


def reference(conv_input, dt_raw, conv_weight, conv_bias, dt_bias, a_log, d_skip, cache_state, cache_tail, hit_slot, hit_mask, suffix_len, write_slot):
    hit_weight = hit_mask.astype(jnp.float32)
    start_state = cache_state[hit_slot].astype(jnp.float32) * hit_weight[:, None, None, None]
    start_tail = cache_tail[hit_slot].astype(jnp.float32) * hit_weight[:, None, None]

    def one_request(request_items):
        results = conv_and_scan(request_items[0], request_items[1], request_items[2], request_items[3], request_items[4], conv_weight, conv_bias, dt_bias, a_log, d_skip)
        return (results[0], results[1], results[2])

    y_all, final_states, tail_all = lax.map(one_request, (conv_input, dt_raw, start_state, start_tail, suffix_len))
    new_state = jnp.zeros(final_states.shape, jnp.bfloat16).at[write_slot].set(final_states.astype(jnp.bfloat16))
    new_tail = jnp.zeros(tail_all.shape, jnp.bfloat16).at[write_slot].set(tail_all.astype(jnp.bfloat16))
    return (y_all.astype(jnp.bfloat16), new_state, new_tail)
```

```python
import jax
import jax.numpy as jnp
from jax import lax
from jax.experimental import pallas as pl
from jax.experimental.pallas import tpu as pltpu
from jax.sharding import PartitionSpec as P

HEADS = 256
HEAD_P = 64
NSTATE = 256
GROUPS = 8
PER_GROUP = HEADS // GROUPS
HB = 8
HBW = HB * HEAD_P
BLOCKS = PER_GROUP // HB
VMEM = 56 * 1024 * 1024

highest = lax.Precision.HIGHEST
f32 = jnp.float32


def dot(a, b, dims):
    return lax.dot_general(a, b, (dims, ((), ())), precision=highest, preferred_element_type=f32)


def conv_silu(scratch, x_ref, tail_ref, w_ref, b_ref):
    steps = x_ref.shape[0]
    scratch[0:8, :] = tail_ref[...]
    scratch[8 : 8 + steps, :] = x_ref[...].astype(f32)
    total = b_ref[...]
    for k in range(4):
        total = total + w_ref[k : k + 1, :] * scratch[5 + k : 5 + k + steps, :]
    return total / (1.0 + jnp.exp(-total))


def widen(cols):
    head = lax.broadcasted_iota(jnp.int32, (HB, HBW), 0)
    lane = lax.broadcasted_iota(jnp.int32, (HB, HBW), 1)
    spread = jnp.where(lane // HEAD_P == head, 1.0, 0.0).astype(f32)
    return dot(cols, spread, ((1,), (0,)))


def scan_kernel(
    x_ref, bc_ref, tailx_ref, tailbc_ref, wx_ref, wbc_ref, bx_ref, bbc_ref,
    step_ref, cum_ref, cumt_ref, skip_ref,
    y_ref, c_ref, add_ref,
    scratch, b_s, cb_s,
):
    steps = x_ref.shape[0]

    @pl.when(pl.program_id(1) == 0)
    def _():
        bc = conv_silu(scratch, bc_ref, tailbc_ref, wbc_ref, bbc_ref)
        b_s[...] = bc[:, :NSTATE]
        c_ref[...] = bc[:, NSTATE:]
        cb = dot(bc[:, NSTATE:], bc[:, :NSTATE], ((1,), (1,)))
        row = lax.broadcasted_iota(jnp.int32, (steps, steps), 0)
        col = lax.broadcasted_iota(jnp.int32, (steps, steps), 1)
        cb_s[...] = jnp.where(row >= col, cb, 0.0)

    x = conv_silu(scratch, x_ref, tailx_ref, wx_ref, bx_ref)
    cum = cum_ref[0]
    x_scaled = x * widen(step_ref[0])
    x_tail = x_scaled * widen(jnp.exp(cum[steps - 1 : steps, :] - cum))
    add = dot(x_tail, b_s[...], ((0,), (0,)))
    add_ref[...] = add.reshape(HB, HEAD_P, NSTATE)
    lane = lax.broadcasted_iota(jnp.int32, (steps, 2 * HEAD_P), 1)
    for pair in range(HB // 2):
        lo, hi = pair * 2 * HEAD_P, (pair + 1) * 2 * HEAD_P
        both = x_scaled[:, lo:hi]
        parts = []
        for k in (2 * pair, 2 * pair + 1):
            gap = jnp.minimum(cum[:, k : k + 1] - cumt_ref[k : k + 1, :], 0.0)
            parts.append(dot(jnp.exp(gap) * cb_s[...], both, ((1,), (0,))))
        inner = jnp.where(lane < HEAD_P, parts[0], parts[1])
        y_ref[:, lo:hi] = inner + skip_ref[:, lo:hi] * x[:, lo:hi]


def prefix_kernel(len_ref, y_ref, c_ref, cum_ref, state_ref, out_ref):
    steps = y_ref.shape[0]
    state = state_ref[...].reshape(HBW, NSTATE).astype(f32)
    carried = dot(c_ref[...], state, ((1,), (1,)))
    total = y_ref[...] + carried * widen(jnp.exp(cum_ref[0]))
    row = lax.broadcasted_iota(jnp.int32, (steps, HBW), 0)
    out_ref[...] = jnp.where(row < len_ref[0], total, 0.0).astype(jnp.bfloat16)


def final_kernel(decay_ref, add_ref, state_ref, out_ref):
    base = pl.program_id(0) * HB
    for k in range(HB):
        out_ref[k] = (
            decay_ref[base + k] * state_ref[k].astype(f32) + add_ref[k]
        ).astype(jnp.bfloat16)


def choose_kernel(slot_ref, mask_ref, in_ref, out_ref):
    keep = mask_ref[pl.program_id(0)] > 0
    out_ref[...] = jnp.where(keep, in_ref[...], jnp.zeros_like(in_ref))


def choose(parts, slot, mask):
    count = parts.shape[0]
    block = (1,) + parts.shape[1:]
    return pl.pallas_call(
        choose_kernel,
        grid_spec=pltpu.PrefetchScalarGridSpec(
            num_scalar_prefetch=2,
            grid=(count,),
            in_specs=[pl.BlockSpec(block, lambda r, s, m: (s[r], 0, 0, 0))],
            out_specs=pl.BlockSpec(block, lambda r, s, m: (r, 0, 0, 0)),
        ),
        out_shape=jax.ShapeDtypeStruct(parts.shape, parts.dtype),
        compiler_params=pltpu.CompilerParams(vmem_limit_bytes=VMEM),
        cost_estimate=pl.CostEstimate(flops=0, bytes_accessed=4 * parts.size, transcendentals=0),
    )(slot, mask, parts)


def move_state(state, slot, mask):
    n = lax.axis_size("cache")
    pieces = state.reshape(n, state.shape[0] // n, HEAD_P, NSTATE)
    parts = lax.all_to_all(pieces, "cache", split_axis=0, concat_axis=0, tiled=True)
    chosen = choose(parts, slot, mask)
    return lax.all_to_all(chosen, "cache", split_axis=0, concat_axis=0, tiled=True).reshape(
        state.shape
    )


def per_device(
    conv_input, dt_raw, conv_weight, conv_bias, dt_bias, a_log, d_skip,
    cache_state, cache_tail, hit_slot, hit_mask, suffix_len, write_slot,
):
    conv = conv_input[0]
    steps, channels = conv.shape
    heads = dt_raw.shape[2]
    tail_count = cache_tail.shape[1]
    groups_here = heads // PER_GROUP
    blocks = groups_here * BLOCKS
    n = lax.axis_size("cache")
    me = lax.axis_index("cache")

    new_tail = lax.dynamic_slice_in_dim(conv, suffix_len[0] - tail_count, tail_count, 0)
    ints = jnp.concatenate([hit_slot, hit_mask, write_slot]).astype(jnp.bfloat16)
    row = jnp.concatenate(
        [
            cache_tail.reshape(-1, 128),
            new_tail.reshape(-1, 128),
            jnp.pad(ints, (0, 125)).reshape(1, 128),
        ],
        axis=0,
    )
    rows = lax.all_to_all(
        jnp.broadcast_to(row[None], (n,) + row.shape), "cache", split_axis=0, concat_axis=0,
        tiled=True,
    )
    table = rows[:, -1, :3].astype(jnp.int32)
    all_slot, all_mask, all_write = table[:, 0], table[:, 1], table[:, 2]
    ids = jnp.arange(n, dtype=jnp.int32)
    inverse = jnp.sum(jnp.where(all_write[None, :] == ids[:, None], ids[None, :], 0), axis=1)
    tail_rows = tail_count * channels // 128
    start_tail = lax.dynamic_index_in_dim(rows[:, :tail_rows], hit_slot[0], 0, keepdims=False)
    start_tail = jnp.where(hit_mask[0] > 0, start_tail, jnp.zeros((), jnp.bfloat16))
    start_tail = start_tail.reshape(tail_count, channels).astype(f32)
    tail8 = jnp.pad(start_tail, ((8 - tail_count, 0), (0, 0)))
    out_tail = lax.dynamic_index_in_dim(
        rows[:, tail_rows : 2 * tail_rows], inverse[me], 0, keepdims=False
    ).reshape(1, tail_count, channels)

    position = lax.broadcasted_iota(jnp.int32, (steps, 1), 0)
    step = jax.nn.softplus(dt_raw[0] + dt_bias[None, :]) * (position < suffix_len[0]).astype(f32)
    cum = jnp.cumsum(step * (-jnp.exp(a_log))[None, :], axis=0)
    step_b = step.reshape(steps, blocks, HB).transpose(1, 0, 2)
    cum_b = cum.reshape(steps, blocks, HB).transpose(1, 0, 2)
    end_decay = jnp.exp(cum[-1])
    skip_wide = jnp.repeat(d_skip, HEAD_P).reshape(1, heads * HEAD_P)
    bias = conv_bias.reshape(1, channels)

    wide = BLOCKS + 1

    def xs(rows_):
        return pl.BlockSpec((rows_, HBW), lambda g, b: (0, g * wide + b))

    def bcs(rows_):
        return pl.BlockSpec((rows_, HBW), lambda g, b: (0, g * wide + BLOCKS))

    per_block = pl.BlockSpec((1, steps, HB), lambda g, b: (g * BLOCKS + b, 0, 0))
    y_part, c_rows, add = pl.pallas_call(
        scan_kernel,
        grid=(groups_here, BLOCKS),
        in_specs=[
            xs(steps), bcs(steps), xs(8), bcs(8), xs(4), bcs(4), xs(1), bcs(1),
            per_block, per_block,
            pl.BlockSpec((HB, steps), lambda g, b: (g * BLOCKS + b, 0)),
            pl.BlockSpec((1, HBW), lambda g, b: (0, g * BLOCKS + b)),
        ],
        out_specs=[
            pl.BlockSpec((steps, HBW), lambda g, b: (0, g * BLOCKS + b)),
            pl.BlockSpec((steps, NSTATE), lambda g, b: (0, g)),
            pl.BlockSpec((HB, HEAD_P, NSTATE), lambda g, b: (g * BLOCKS + b, 0, 0)),
        ],
        out_shape=[
            jax.ShapeDtypeStruct((steps, heads * HEAD_P), f32),
            jax.ShapeDtypeStruct((steps, groups_here * NSTATE), f32),
            jax.ShapeDtypeStruct((heads, HEAD_P, NSTATE), f32),
        ],
        scratch_shapes=[
            pltpu.VMEM((steps + 8, HBW), f32),
            pltpu.VMEM((steps, NSTATE), f32),
            pltpu.VMEM((steps, steps), f32),
        ],
        compiler_params=pltpu.CompilerParams(vmem_limit_bytes=VMEM),
        cost_estimate=pl.CostEstimate(
            flops=20_000_000_000, bytes_accessed=12_000_000, transcendentals=6_000_000
        ),
    )(
        conv, conv, tail8, tail8, conv_weight, conv_weight, bias, bias,
        step_b, cum_b, cum.T, skip_wide,
    )

    start_state = move_state(cache_state[0], all_slot, all_mask)

    final = pl.pallas_call(
        final_kernel,
        grid=(blocks,),
        in_specs=[
            pl.BlockSpec(memory_space=pltpu.SMEM),
            pl.BlockSpec((HB, HEAD_P, NSTATE), lambda b: (b, 0, 0)),
            pl.BlockSpec((HB, HEAD_P, NSTATE), lambda b: (b, 0, 0)),
        ],
        out_specs=pl.BlockSpec((HB, HEAD_P, NSTATE), lambda b: (b, 0, 0)),
        out_shape=jax.ShapeDtypeStruct((heads, HEAD_P, NSTATE), jnp.bfloat16),
        compiler_params=pltpu.CompilerParams(vmem_limit_bytes=VMEM),
        cost_estimate=pl.CostEstimate(flops=2_000_000, bytes_accessed=8_000_000, transcendentals=0),
    )(end_decay, add, start_state)

    owned = move_state(final, inverse, jnp.ones((n,), jnp.int32))

    y = pl.pallas_call(
        prefix_kernel,
        grid=(blocks,),
        in_specs=[
            pl.BlockSpec(memory_space=pltpu.SMEM),
            pl.BlockSpec((steps, HBW), lambda b: (0, b)),
            pl.BlockSpec((steps, NSTATE), lambda b: (0, b // BLOCKS)),
            pl.BlockSpec((1, steps, HB), lambda b: (b, 0, 0)),
            pl.BlockSpec((HB, HEAD_P, NSTATE), lambda b: (b, 0, 0)),
        ],
        out_specs=pl.BlockSpec((steps, HBW), lambda b: (0, b)),
        out_shape=jax.ShapeDtypeStruct((steps, heads * HEAD_P), jnp.bfloat16),
        compiler_params=pltpu.CompilerParams(vmem_limit_bytes=VMEM),
        cost_estimate=pl.CostEstimate(
            flops=6_000_000_000, bytes_accessed=9_000_000, transcendentals=100_000
        ),
    )(suffix_len, y_part, c_rows, cum_b, start_state)
    return y[None], owned[None], out_tail


def solution(mesh):
    placed = (
        P(("groups", "cache"), None, ("mp", "sub")),
        P(("groups", "cache"), None, ("mp", "sub")),
        P(None, ("mp", "sub")),
        P(("mp", "sub")),
        P(("mp", "sub")),
        P(("mp", "sub")),
        P(("mp", "sub")),
        P(("groups", "cache"), ("mp", "sub"), None, None),
        P(("groups", "cache"), None, ("mp", "sub")),
        P(("groups", "cache")),
        P(("groups", "cache")),
        P(("groups", "cache")),
        P(("groups", "cache")),
    )
    return jax.shard_map(
        per_device,
        mesh=mesh,
        in_specs=placed,
        out_specs=(
            P(("groups", "cache"), None, ("mp", "sub")),
            P(("groups", "cache"), ("mp", "sub"), None, None),
            P(("groups", "cache"), None, ("mp", "sub")),
        ),
        check_vma=False,
    )
```

```python
import functools

import jax
import jax.numpy as jnp
from jax import lax
from jax.experimental import pallas as pl
from jax.experimental.pallas import tpu as pltpu
from jax.sharding import PartitionSpec as P

HEADS = 256
HEAD_P = 64
NSTATE = 256
GROUPS = 8
PER_GROUP = HEADS // GROUPS
HB = 8
HBW = HB * HEAD_P
BLOCKS = PER_GROUP // HB
VMEM = 56 * 1024 * 1024

highest = lax.Precision.HIGHEST
f32 = jnp.float32
MESH = pl.DeviceIdType.MESH
LINE = 4
CHUNKS = 16


def dot(a, b, dims):
    return lax.dot_general(a, b, (dims, ((), ())), precision=highest, preferred_element_type=f32)


def conv_silu(scratch, x_ref, tail_ref, w_ref, b_ref):
    steps = x_ref.shape[0]
    scratch[0:8, :] = tail_ref[...]
    scratch[8 : 8 + steps, :] = x_ref[...].astype(f32)
    total = b_ref[...]
    for k in range(4):
        total = total + w_ref[k : k + 1, :] * scratch[5 + k : 5 + k + steps, :]
    return total / (1.0 + jnp.exp(-total))


def widen(cols):
    head = lax.broadcasted_iota(jnp.int32, (HB, HBW), 0)
    lane = lax.broadcasted_iota(jnp.int32, (HB, HBW), 1)
    spread = jnp.where(lane // HEAD_P == head, 1.0, 0.0).astype(f32)
    return dot(cols, spread, ((1,), (0,)))


def scan_kernel(
    x_ref, bc_ref, tailx_ref, tailbc_ref, wx_ref, wbc_ref, bx_ref, bbc_ref,
    step_ref, cum_ref, cumt_ref, skip_ref,
    y_ref, c_ref, add_ref,
    scratch, b_s, cb_s,
):
    steps = x_ref.shape[0]

    @pl.when(pl.program_id(1) == 0)
    def _():
        bc = conv_silu(scratch, bc_ref, tailbc_ref, wbc_ref, bbc_ref)
        b_s[...] = bc[:, :NSTATE]
        c_ref[...] = bc[:, NSTATE:]
        cb = dot(bc[:, NSTATE:], bc[:, :NSTATE], ((1,), (1,)))
        row = lax.broadcasted_iota(jnp.int32, (steps, steps), 0)
        col = lax.broadcasted_iota(jnp.int32, (steps, steps), 1)
        cb_s[...] = jnp.where(row >= col, cb, 0.0)

    x = conv_silu(scratch, x_ref, tailx_ref, wx_ref, bx_ref)
    cum = cum_ref[0]
    x_scaled = x * widen(step_ref[0])
    x_tail = x_scaled * widen(jnp.exp(cum[steps - 1 : steps, :] - cum))
    add = dot(x_tail, b_s[...], ((0,), (0,)))
    add_ref[...] = add.reshape(HB, HEAD_P, NSTATE)
    lane = lax.broadcasted_iota(jnp.int32, (steps, 2 * HEAD_P), 1)
    for pair in range(HB // 2):
        lo, hi = pair * 2 * HEAD_P, (pair + 1) * 2 * HEAD_P
        both = x_scaled[:, lo:hi]
        parts = []
        for k in (2 * pair, 2 * pair + 1):
            gap = jnp.minimum(cum[:, k : k + 1] - cumt_ref[k : k + 1, :], 0.0)
            parts.append(dot(jnp.exp(gap) * cb_s[...], both, ((1,), (0,))))
        inner = jnp.where(lane < HEAD_P, parts[0], parts[1])
        y_ref[:, lo:hi] = inner + skip_ref[:, lo:hi] * x[:, lo:hi]


def prefix_kernel(len_ref, y_ref, c_ref, cum_ref, state_ref, out_ref):
    steps = y_ref.shape[0]
    state = state_ref[...].reshape(HBW, NSTATE).astype(f32)
    carried = dot(c_ref[...], state, ((1,), (1,)))
    total = y_ref[...] + carried * widen(jnp.exp(cum_ref[0]))
    row = lax.broadcasted_iota(jnp.int32, (steps, HBW), 0)
    out_ref[...] = jnp.where(row < len_ref[0], total, 0.0).astype(jnp.bfloat16)


def final_kernel(decay_ref, add_ref, state_ref, out_ref):
    base = pl.program_id(0) * HB
    for k in range(HB):
        out_ref[k] = (
            decay_ref[base + k] * state_ref[k].astype(f32) + add_ref[k]
        ).astype(jnp.bfloat16)


def choose_kernel(slot_ref, mask_ref, in_ref, out_ref):
    keep = mask_ref[pl.program_id(0)] > 0
    out_ref[...] = jnp.where(keep, in_ref[...], jnp.zeros_like(in_ref))


def choose(parts, slot, mask):
    count = parts.shape[0]
    block = (1,) + parts.shape[1:]
    return pl.pallas_call(
        choose_kernel,
        grid_spec=pltpu.PrefetchScalarGridSpec(
            num_scalar_prefetch=2,
            grid=(count,),
            in_specs=[pl.BlockSpec(block, lambda r, s, m: (s[r], 0, 0, 0))],
            out_specs=pl.BlockSpec(block, lambda r, s, m: (r, 0, 0, 0)),
        ),
        out_shape=jax.ShapeDtypeStruct(parts.shape, parts.dtype),
        compiler_params=pltpu.CompilerParams(vmem_limit_bytes=VMEM),
        cost_estimate=pl.CostEstimate(flops=0, bytes_accessed=4 * parts.size, transcendentals=0),
    )(slot, mask, parts)


def move_state(state, slot, mask):
    n = lax.axis_size("cache")
    pieces = state.reshape(n, state.shape[0] // n, HEAD_P, NSTATE)
    parts = lax.all_to_all(pieces, "cache", split_axis=0, concat_axis=0, tiled=True)
    chosen = choose(parts, slot, mask)
    return lax.all_to_all(chosen, "cache", split_axis=0, concat_axis=0, tiled=True).reshape(
        state.shape
    )


def relay_kernel(
    n, chunks, pick_ref, own_ref, out_ref,
    right_in, left_in, right_out, left_out, send_r, recv_r, send_l, recv_l,
):
    me = lax.axis_index("cache")
    per = own_ref.shape[0] // chunks
    first, last = me == 0, me == n - 1
    barrier = pltpu.get_barrier_semaphore()

    @pl.when(jnp.logical_not(first))
    def _():
        pl.semaphore_signal(barrier, inc=1, device_id={"cache": me - 1}, device_id_type=MESH)

    @pl.when(jnp.logical_not(last))
    def _():
        pl.semaphore_signal(barrier, inc=1, device_id={"cache": me + 1}, device_id_type=MESH)

    @pl.when(jnp.logical_or(first, last))
    def _():
        pl.semaphore_wait(barrier, 1)

    @pl.when(jnp.logical_not(jnp.logical_or(first, last)))
    def _():
        pl.semaphore_wait(barrier, 2)

    def go_right(c, src):
        return pltpu.make_async_remote_copy(
            src_ref=src.at[pl.ds(c * per, per)], dst_ref=right_in.at[pl.ds(c * per, per)],
            send_sem=send_r.at[c], recv_sem=recv_r.at[c],
            device_id={"cache": lax.rem(me + 1, n)}, device_id_type=MESH,
        )

    def go_left(c, src):
        return pltpu.make_async_remote_copy(
            src_ref=src.at[pl.ds(c * per, per)], dst_ref=left_in.at[pl.ds(c * per, per)],
            send_sem=send_l.at[c], recv_sem=recv_l.at[c],
            device_id={"cache": lax.rem(me + n - 1, n)}, device_id_type=MESH,
        )

    @pl.when(first)
    def _():
        @pl.loop(0, chunks)
        def _(c):
            go_right(c, own_ref).start()

    @pl.when(last)
    def _():
        @pl.loop(0, chunks)
        def _(c):
            go_left(c, own_ref).start()

    @pl.loop(0, chunks + n - 1)
    def _(s):
        cr = s - me
        cl = s - (n - 1 - me)

        @pl.when(jnp.logical_and(jnp.logical_not(first), jnp.logical_and(cr >= 0, cr < chunks)))
        def _():
            go_right(cr, own_ref).wait_recv()

            @pl.when(jnp.logical_not(last))
            def _():
                at = pl.ds(cr * per, per)
                right_out[at] = jnp.where(pick_ref[0] > 0, own_ref[at], right_in[at])
                go_right(cr, right_out).start()

        @pl.when(jnp.logical_and(jnp.logical_not(last), jnp.logical_and(cl >= 0, cl < chunks)))
        def _():
            go_left(cl, own_ref).wait_recv()

            @pl.when(jnp.logical_not(first))
            def _():
                at = pl.ds(cl * per, per)
                left_out[at] = jnp.where(pick_ref[1] > 0, own_ref[at], left_in[at])
                go_left(cl, left_out).start()

    def result(low, high):
        @pl.loop(0, chunks)
        def _(c):
            at = pl.ds(c * per, per)
            value = own_ref[at]
            if low:
                value = jnp.where(pick_ref[2] > 0, right_in[at], value)
            if high:
                value = jnp.where(pick_ref[3] > 0, left_in[at], value)
            out_ref[at] = jnp.where(pick_ref[4] > 0, value, jnp.zeros_like(value))

    @pl.when(first)
    def _():
        result(False, True)

    @pl.when(last)
    def _():
        result(True, False)

    @pl.when(jnp.logical_not(jnp.logical_or(first, last)))
    def _():
        result(True, True)

    @pl.when(jnp.logical_not(last))
    def _():
        @pl.loop(0, chunks)
        def _(c):
            go_right(c, own_ref).wait_send()

    @pl.when(jnp.logical_not(first))
    def _():
        @pl.loop(0, chunks)
        def _(c):
            go_left(c, own_ref).wait_send()


def relay(state, picks):
    n = lax.axis_size("cache")
    chunks = min(CHUNKS, state.shape[0])
    vmem = pl.BlockSpec(memory_space=pltpu.VMEM)
    return pl.pallas_call(
        functools.partial(relay_kernel, n, chunks),
        in_specs=[pl.BlockSpec(memory_space=pltpu.SMEM), vmem],
        out_specs=vmem,
        out_shape=jax.ShapeDtypeStruct(state.shape, state.dtype),
        scratch_shapes=[pltpu.VMEM(state.shape, state.dtype)] * 4
        + [pltpu.SemaphoreType.DMA((chunks,))] * 4,
        compiler_params=pltpu.CompilerParams(
            collective_id=0, has_side_effects=True, vmem_limit_bytes=32 * 1024 * 1024
        ),
        cost_estimate=pl.CostEstimate(
            flops=0, bytes_accessed=100_000_000, transcendentals=0
        ),
    )(picks, state)


def relay_plan(slot, mask):
    n = lax.axis_size("cache")
    me = lax.axis_index("cache")
    ids = jnp.arange(n, dtype=jnp.int32)
    wants = (slot[None, :] == ids[:, None]) & (mask[None, :] > 0)
    right_of = ids[None, :] > ids[:, None]
    right = jnp.any(wants[:, None, :] & right_of[None], axis=2) & (ids[:, None] <= ids[None, :])
    left = jnp.any(wants[:, None, :] & right_of.T[None], axis=2) & (ids[:, None] >= ids[None, :])
    most = jnp.maximum(
        jnp.max(jnp.sum(right.astype(jnp.int32), axis=0)),
        jnp.max(jnp.sum(left.astype(jnp.int32), axis=0)),
    )
    mine = slot[me]
    picks = jnp.stack([right[me, me], left[me, me], mine < me, mine > me, mask[me] > 0])
    return picks.astype(jnp.int32), most


def per_device(
    conv_input, dt_raw, conv_weight, conv_bias, dt_bias, a_log, d_skip,
    cache_state, cache_tail, hit_slot, hit_mask, suffix_len, write_slot,
):
    conv = conv_input[0]
    steps, channels = conv.shape
    heads = dt_raw.shape[2]
    tail_count = cache_tail.shape[1]
    groups_here = heads // PER_GROUP
    blocks = groups_here * BLOCKS
    n = lax.axis_size("cache")
    me = lax.axis_index("cache")

    new_tail = lax.dynamic_slice_in_dim(conv, suffix_len[0] - tail_count, tail_count, 0)
    ints = jnp.concatenate([hit_slot, hit_mask, write_slot]).astype(jnp.bfloat16)
    row = jnp.concatenate(
        [
            cache_tail.reshape(-1, 128),
            new_tail.reshape(-1, 128),
            jnp.pad(ints, (0, 125)).reshape(1, 128),
        ],
        axis=0,
    )
    if n <= LINE:
        steps_by = [row] + [
            lax.ppermute(row, "cache", [(i, (i + shift) % n) for i in range(n)])
            for shift in range(1, n)
        ]
        came = jnp.stack(steps_by)
        rows = jnp.stack(
            [lax.dynamic_index_in_dim(came, (me - i) % n, 0, keepdims=False) for i in range(n)]
        )
    else:
        rows = lax.all_to_all(
            jnp.broadcast_to(row[None], (n,) + row.shape), "cache", split_axis=0, concat_axis=0,
            tiled=True,
        )
    table = rows[:, -1, :3].astype(jnp.int32)
    all_slot, all_mask, all_write = table[:, 0], table[:, 1], table[:, 2]
    ids = jnp.arange(n, dtype=jnp.int32)
    inverse = jnp.sum(jnp.where(all_write[None, :] == ids[:, None], ids[None, :], 0), axis=1)
    tail_rows = tail_count * channels // 128
    start_tail = lax.dynamic_index_in_dim(rows[:, :tail_rows], hit_slot[0], 0, keepdims=False)
    start_tail = jnp.where(hit_mask[0] > 0, start_tail, jnp.zeros((), jnp.bfloat16))
    start_tail = start_tail.reshape(tail_count, channels).astype(f32)
    tail8 = jnp.pad(start_tail, ((8 - tail_count, 0), (0, 0)))
    out_tail = lax.dynamic_index_in_dim(
        rows[:, tail_rows : 2 * tail_rows], inverse[me], 0, keepdims=False
    ).reshape(1, tail_count, channels)

    position = lax.broadcasted_iota(jnp.int32, (steps, 1), 0)
    step = jax.nn.softplus(dt_raw[0] + dt_bias[None, :]) * (position < suffix_len[0]).astype(f32)
    cum = jnp.cumsum(step * (-jnp.exp(a_log))[None, :], axis=0)
    step_b = step.reshape(steps, blocks, HB).transpose(1, 0, 2)
    cum_b = cum.reshape(steps, blocks, HB).transpose(1, 0, 2)
    end_decay = jnp.exp(cum[-1])
    skip_wide = jnp.repeat(d_skip, HEAD_P).reshape(1, heads * HEAD_P)
    bias = conv_bias.reshape(1, channels)

    wide = BLOCKS + 1

    def xs(rows_):
        return pl.BlockSpec((rows_, HBW), lambda g, b: (0, g * wide + b))

    def bcs(rows_):
        return pl.BlockSpec((rows_, HBW), lambda g, b: (0, g * wide + BLOCKS))

    per_block = pl.BlockSpec((1, steps, HB), lambda g, b: (g * BLOCKS + b, 0, 0))
    y_part, c_rows, add = pl.pallas_call(
        scan_kernel,
        grid=(groups_here, BLOCKS),
        in_specs=[
            xs(steps), bcs(steps), xs(8), bcs(8), xs(4), bcs(4), xs(1), bcs(1),
            per_block, per_block,
            pl.BlockSpec((HB, steps), lambda g, b: (g * BLOCKS + b, 0)),
            pl.BlockSpec((1, HBW), lambda g, b: (0, g * BLOCKS + b)),
        ],
        out_specs=[
            pl.BlockSpec((steps, HBW), lambda g, b: (0, g * BLOCKS + b)),
            pl.BlockSpec((steps, NSTATE), lambda g, b: (0, g)),
            pl.BlockSpec((HB, HEAD_P, NSTATE), lambda g, b: (g * BLOCKS + b, 0, 0)),
        ],
        out_shape=[
            jax.ShapeDtypeStruct((steps, heads * HEAD_P), f32),
            jax.ShapeDtypeStruct((steps, groups_here * NSTATE), f32),
            jax.ShapeDtypeStruct((heads, HEAD_P, NSTATE), f32),
        ],
        scratch_shapes=[
            pltpu.VMEM((steps + 8, HBW), f32),
            pltpu.VMEM((steps, NSTATE), f32),
            pltpu.VMEM((steps, steps), f32),
        ],
        compiler_params=pltpu.CompilerParams(vmem_limit_bytes=VMEM),
        cost_estimate=pl.CostEstimate(
            flops=20_000_000_000, bytes_accessed=12_000_000, transcendentals=6_000_000
        ),
    )(
        conv, conv, tail8, tail8, conv_weight, conv_weight, bias, bias,
        step_b, cum_b, cum.T, skip_wide,
    )

    start_state = move_state(cache_state[0], all_slot, all_mask)

    final = pl.pallas_call(
        final_kernel,
        grid=(blocks,),
        in_specs=[
            pl.BlockSpec(memory_space=pltpu.SMEM),
            pl.BlockSpec((HB, HEAD_P, NSTATE), lambda b: (b, 0, 0)),
            pl.BlockSpec((HB, HEAD_P, NSTATE), lambda b: (b, 0, 0)),
        ],
        out_specs=pl.BlockSpec((HB, HEAD_P, NSTATE), lambda b: (b, 0, 0)),
        out_shape=jax.ShapeDtypeStruct((heads, HEAD_P, NSTATE), jnp.bfloat16),
        compiler_params=pltpu.CompilerParams(vmem_limit_bytes=VMEM),
        cost_estimate=pl.CostEstimate(flops=2_000_000, bytes_accessed=8_000_000, transcendentals=0),
    )(end_decay, add, start_state)

    def prefix(start):
        return pl.pallas_call(
            prefix_kernel,
            grid=(blocks,),
            in_specs=[
                pl.BlockSpec(memory_space=pltpu.SMEM),
                pl.BlockSpec((steps, HBW), lambda b: (0, b)),
                pl.BlockSpec((steps, NSTATE), lambda b: (0, b // BLOCKS)),
                pl.BlockSpec((1, steps, HB), lambda b: (b, 0, 0)),
                pl.BlockSpec((HB, HEAD_P, NSTATE), lambda b: (b, 0, 0)),
            ],
            out_specs=pl.BlockSpec((steps, HBW), lambda b: (0, b)),
            out_shape=jax.ShapeDtypeStruct((steps, heads * HEAD_P), jnp.bfloat16),
            compiler_params=pltpu.CompilerParams(vmem_limit_bytes=VMEM),
            cost_estimate=pl.CostEstimate(
                flops=6_000_000_000, bytes_accessed=9_000_000, transcendentals=100_000
            ),
        )(suffix_len, y_part, c_rows, cum_b, start)

    def two_phase(final, start):
        return move_state(final, inverse, ones), prefix(start)

    def along_line(final, start):
        return relay(final, picks), prefix(start)

    ones = jnp.ones((n,), jnp.int32)
    if n <= LINE:
        picks, most = relay_plan(inverse, ones)
        count = lax.axis_size("groups")
        here = most
        for shift in range(1, count):
            ring = [(i, (i + shift) % count) for i in range(count)]
            most = jnp.maximum(most, lax.ppermute(here, "groups", ring))
        owned, y = lax.cond(most <= 1, along_line, two_phase, final, start_state)
    else:
        owned, y = two_phase(final, start_state)
    return y[None], owned[None], out_tail


def solution(mesh):
    placed = (
        P(("groups", "cache"), None, ("mp", "sub")),
        P(("groups", "cache"), None, ("mp", "sub")),
        P(None, ("mp", "sub")),
        P(("mp", "sub")),
        P(("mp", "sub")),
        P(("mp", "sub")),
        P(("mp", "sub")),
        P(("groups", "cache"), ("mp", "sub"), None, None),
        P(("groups", "cache"), None, ("mp", "sub")),
        P(("groups", "cache")),
        P(("groups", "cache")),
        P(("groups", "cache")),
        P(("groups", "cache")),
    )
    return jax.shard_map(
        per_device,
        mesh=mesh,
        in_specs=placed,
        out_specs=(
            P(("groups", "cache"), None, ("mp", "sub")),
            P(("groups", "cache"), ("mp", "sub"), None, None),
            P(("groups", "cache"), None, ("mp", "sub")),
        ),
        check_vma=False,
    )
```

```python
import functools

import jax
import jax.numpy as jnp
from jax import lax
from jax.experimental import pallas as pl
from jax.experimental.pallas import tpu as pltpu
from jax.sharding import PartitionSpec as P

HEADS = 256
HEAD_P = 64
NSTATE = 256
GROUPS = 8
PER_GROUP = HEADS // GROUPS
HB = 8
HBW = HB * HEAD_P
BLOCKS = PER_GROUP // HB
VMEM = 56 * 1024 * 1024

highest = lax.Precision.HIGHEST
f32 = jnp.float32
MESH = pl.DeviceIdType.MESH
LINE = 4
CHUNKS = 16


def dot(a, b, dims):
    return lax.dot_general(a, b, (dims, ((), ())), precision=highest, preferred_element_type=f32)


def conv_silu(scratch, x_ref, tail_ref, w_ref, b_ref):
    steps = x_ref.shape[0]
    scratch[0:8, :] = tail_ref[...]
    scratch[8 : 8 + steps, :] = x_ref[...].astype(f32)
    total = b_ref[...]
    for k in range(4):
        total = total + w_ref[k : k + 1, :] * scratch[5 + k : 5 + k + steps, :]
    return total / (1.0 + jnp.exp(-total))


def widen(cols):
    head = lax.broadcasted_iota(jnp.int32, (HB, HBW), 0)
    lane = lax.broadcasted_iota(jnp.int32, (HB, HBW), 1)
    spread = jnp.where(lane // HEAD_P == head, 1.0, 0.0).astype(f32)
    return dot(cols, spread, ((1,), (0,)))


def scan_kernel(
    x_ref, bc_ref, tailx_ref, tailbc_ref, wx_ref, wbc_ref, bx_ref, bbc_ref,
    step_ref, cum_ref, cumt_ref, skip_ref,
    y_ref, c_ref, add_ref,
    scratch, b_s, cb_s,
):
    steps = x_ref.shape[0]

    @pl.when(pl.program_id(1) == 0)
    def _():
        bc = conv_silu(scratch, bc_ref, tailbc_ref, wbc_ref, bbc_ref)
        b_s[...] = bc[:, :NSTATE]
        c_ref[...] = bc[:, NSTATE:]
        cb = dot(bc[:, NSTATE:], bc[:, :NSTATE], ((1,), (1,)))
        row = lax.broadcasted_iota(jnp.int32, (steps, steps), 0)
        col = lax.broadcasted_iota(jnp.int32, (steps, steps), 1)
        cb_s[...] = jnp.where(row >= col, cb, 0.0)

    x = conv_silu(scratch, x_ref, tailx_ref, wx_ref, bx_ref)
    cum = cum_ref[0]
    x_scaled = x * widen(step_ref[0])
    x_tail = x_scaled * widen(jnp.exp(cum[steps - 1 : steps, :] - cum))
    add = dot(x_tail, b_s[...], ((0,), (0,)))
    add_ref[...] = add.reshape(HB, HEAD_P, NSTATE)
    lane = lax.broadcasted_iota(jnp.int32, (steps, 2 * HEAD_P), 1)
    for pair in range(HB // 2):
        lo, hi = pair * 2 * HEAD_P, (pair + 1) * 2 * HEAD_P
        both = x_scaled[:, lo:hi]
        parts = []
        for k in (2 * pair, 2 * pair + 1):
            gap = jnp.minimum(cum[:, k : k + 1] - cumt_ref[k : k + 1, :], 0.0)
            parts.append(dot(jnp.exp(gap) * cb_s[...], both, ((1,), (0,))))
        inner = jnp.where(lane < HEAD_P, parts[0], parts[1])
        y_ref[:, lo:hi] = inner + skip_ref[:, lo:hi] * x[:, lo:hi]


def prefix_kernel(len_ref, y_ref, c_ref, cum_ref, state_ref, out_ref):
    steps = y_ref.shape[0]
    state = state_ref[...].reshape(HBW, NSTATE).astype(f32)
    carried = dot(c_ref[...], state, ((1,), (1,)))
    total = y_ref[...] + carried * widen(jnp.exp(cum_ref[0]))
    row = lax.broadcasted_iota(jnp.int32, (steps, HBW), 0)
    out_ref[...] = jnp.where(row < len_ref[0], total, 0.0).astype(jnp.bfloat16)


def final_kernel(decay_ref, add_ref, state_ref, out_ref):
    base = pl.program_id(0) * HB
    for k in range(HB):
        out_ref[k] = (
            decay_ref[base + k] * state_ref[k].astype(f32) + add_ref[k]
        ).astype(jnp.bfloat16)


def choose_kernel(slot_ref, mask_ref, in_ref, out_ref):
    keep = mask_ref[pl.program_id(0)] > 0
    out_ref[...] = jnp.where(keep, in_ref[...], jnp.zeros_like(in_ref))


def choose(parts, slot, mask):
    count = parts.shape[0]
    block = (1,) + parts.shape[1:]
    return pl.pallas_call(
        choose_kernel,
        grid_spec=pltpu.PrefetchScalarGridSpec(
            num_scalar_prefetch=2,
            grid=(count,),
            in_specs=[pl.BlockSpec(block, lambda r, s, m: (s[r], 0, 0, 0))],
            out_specs=pl.BlockSpec(block, lambda r, s, m: (r, 0, 0, 0)),
        ),
        out_shape=jax.ShapeDtypeStruct(parts.shape, parts.dtype),
        compiler_params=pltpu.CompilerParams(vmem_limit_bytes=VMEM),
        cost_estimate=pl.CostEstimate(flops=0, bytes_accessed=4 * parts.size, transcendentals=0),
    )(slot, mask, parts)


def move_state(state, slot, mask):
    n = lax.axis_size("cache")
    pieces = state.reshape(n, state.shape[0] // n, HEAD_P, NSTATE)
    parts = lax.all_to_all(pieces, "cache", split_axis=0, concat_axis=0, tiled=True)
    chosen = choose(parts, slot, mask)
    return lax.all_to_all(chosen, "cache", split_axis=0, concat_axis=0, tiled=True).reshape(
        state.shape
    )


def relay_kernel(
    n, chunks, pick_ref, own_ref, out_ref,
    right_in, left_in, right_out, left_out, send_r, recv_r, send_l, recv_l,
):
    me = lax.axis_index("cache")
    per = own_ref.shape[0] // chunks
    first, last = me == 0, me == n - 1
    barrier = pltpu.get_barrier_semaphore()

    @pl.when(jnp.logical_not(first))
    def _():
        pl.semaphore_signal(barrier, inc=1, device_id={"cache": me - 1}, device_id_type=MESH)

    @pl.when(jnp.logical_not(last))
    def _():
        pl.semaphore_signal(barrier, inc=1, device_id={"cache": me + 1}, device_id_type=MESH)

    @pl.when(jnp.logical_or(first, last))
    def _():
        pl.semaphore_wait(barrier, 1)

    @pl.when(jnp.logical_not(jnp.logical_or(first, last)))
    def _():
        pl.semaphore_wait(barrier, 2)

    def go_right(c, src):
        return pltpu.make_async_remote_copy(
            src_ref=src.at[pl.ds(c * per, per)], dst_ref=right_in.at[pl.ds(c * per, per)],
            send_sem=send_r.at[c], recv_sem=recv_r.at[c],
            device_id={"cache": lax.rem(me + 1, n)}, device_id_type=MESH,
        )

    def go_left(c, src):
        return pltpu.make_async_remote_copy(
            src_ref=src.at[pl.ds(c * per, per)], dst_ref=left_in.at[pl.ds(c * per, per)],
            send_sem=send_l.at[c], recv_sem=recv_l.at[c],
            device_id={"cache": lax.rem(me + n - 1, n)}, device_id_type=MESH,
        )

    @pl.when(first)
    def _():
        @pl.loop(0, chunks)
        def _(c):
            go_right(c, own_ref).start()

    @pl.when(last)
    def _():
        @pl.loop(0, chunks)
        def _(c):
            go_left(c, own_ref).start()

    @pl.loop(0, chunks + n - 1)
    def _(s):
        cr = s - me
        cl = s - (n - 1 - me)

        @pl.when(jnp.logical_and(jnp.logical_not(first), jnp.logical_and(cr >= 0, cr < chunks)))
        def _():
            go_right(cr, own_ref).wait_recv()

            @pl.when(jnp.logical_not(last))
            def _():
                at = pl.ds(cr * per, per)
                right_out[at] = jnp.where(pick_ref[0] > 0, own_ref[at], right_in[at])
                go_right(cr, right_out).start()

        @pl.when(jnp.logical_and(jnp.logical_not(last), jnp.logical_and(cl >= 0, cl < chunks)))
        def _():
            go_left(cl, own_ref).wait_recv()

            @pl.when(jnp.logical_not(first))
            def _():
                at = pl.ds(cl * per, per)
                left_out[at] = jnp.where(pick_ref[1] > 0, own_ref[at], left_in[at])
                go_left(cl, left_out).start()

    def result(low, high):
        @pl.loop(0, chunks)
        def _(c):
            at = pl.ds(c * per, per)
            value = own_ref[at]
            if low:
                value = jnp.where(pick_ref[2] > 0, right_in[at], value)
            if high:
                value = jnp.where(pick_ref[3] > 0, left_in[at], value)
            out_ref[at] = jnp.where(pick_ref[4] > 0, value, jnp.zeros_like(value))

    @pl.when(first)
    def _():
        result(False, True)

    @pl.when(last)
    def _():
        result(True, False)

    @pl.when(jnp.logical_not(jnp.logical_or(first, last)))
    def _():
        result(True, True)

    @pl.when(jnp.logical_not(last))
    def _():
        @pl.loop(0, chunks)
        def _(c):
            go_right(c, own_ref).wait_send()

    @pl.when(jnp.logical_not(first))
    def _():
        @pl.loop(0, chunks)
        def _(c):
            go_left(c, own_ref).wait_send()


def relay(state, picks):
    n = lax.axis_size("cache")
    chunks = min(CHUNKS, state.shape[0])
    vmem = pl.BlockSpec(memory_space=pltpu.VMEM)
    return pl.pallas_call(
        functools.partial(relay_kernel, n, chunks),
        in_specs=[pl.BlockSpec(memory_space=pltpu.SMEM), vmem],
        out_specs=vmem,
        out_shape=jax.ShapeDtypeStruct(state.shape, state.dtype),
        scratch_shapes=[pltpu.VMEM(state.shape, state.dtype)] * 4
        + [pltpu.SemaphoreType.DMA((chunks,))] * 4,
        compiler_params=pltpu.CompilerParams(
            collective_id=0, has_side_effects=True, vmem_limit_bytes=32 * 1024 * 1024
        ),
        cost_estimate=pl.CostEstimate(
            flops=0, bytes_accessed=100_000_000, transcendentals=0
        ),
    )(picks, state)


def relay_plan(slot, mask):
    n = lax.axis_size("cache")
    me = lax.axis_index("cache")
    ids = jnp.arange(n, dtype=jnp.int32)
    wants = (slot[None, :] == ids[:, None]) & (mask[None, :] > 0)
    right_of = ids[None, :] > ids[:, None]
    right = jnp.any(wants[:, None, :] & right_of[None], axis=2) & (ids[:, None] <= ids[None, :])
    left = jnp.any(wants[:, None, :] & right_of.T[None], axis=2) & (ids[:, None] >= ids[None, :])
    most = jnp.maximum(
        jnp.max(jnp.sum(right.astype(jnp.int32), axis=0)),
        jnp.max(jnp.sum(left.astype(jnp.int32), axis=0)),
    )
    mine = slot[me]
    picks = jnp.stack([right[me, me], left[me, me], mine < me, mine > me, mask[me] > 0])
    return picks.astype(jnp.int32), most


def to_all(row):
    n = lax.axis_size("cache")
    me = lax.axis_index("cache")
    if n > LINE:
        return lax.all_to_all(
            jnp.broadcast_to(row[None], (n,) + row.shape), "cache", split_axis=0, concat_axis=0,
            tiled=True,
        )
    came = jnp.stack(
        [row]
        + [
            lax.ppermute(row, "cache", [(i, (i + shift) % n) for i in range(n)])
            for shift in range(1, n)
        ]
    )
    return jnp.stack(
        [lax.dynamic_index_in_dim(came, (me - i) % n, 0, keepdims=False) for i in range(n)]
    )


def per_device(
    conv_input, dt_raw, conv_weight, conv_bias, dt_bias, a_log, d_skip,
    cache_state, cache_tail, hit_slot, hit_mask, suffix_len, write_slot,
):
    conv = conv_input[0]
    steps, channels = conv.shape
    heads = dt_raw.shape[2]
    tail_count = cache_tail.shape[1]
    groups_here = heads // PER_GROUP
    blocks = groups_here * BLOCKS
    n = lax.axis_size("cache")
    me = lax.axis_index("cache")

    ints = jnp.concatenate([hit_slot, hit_mask, write_slot])
    table = to_all(ints)
    slots, dt_bias, suffix_len, table = lax.optimization_barrier(
        (cache_state, dt_bias, suffix_len, table)
    )
    new_tail = lax.dynamic_slice_in_dim(conv, suffix_len[0] - tail_count, tail_count, 0)
    row = jnp.concatenate([cache_tail.reshape(-1, 128), new_tail.reshape(-1, 128)], axis=0)
    rows = to_all(row)
    all_slot, all_mask, all_write = table[:, 0], table[:, 1], table[:, 2]
    ids = jnp.arange(n, dtype=jnp.int32)
    inverse = jnp.sum(jnp.where(all_write[None, :] == ids[:, None], ids[None, :], 0), axis=1)
    tail_rows = tail_count * channels // 128
    start_tail = lax.dynamic_index_in_dim(rows[:, :tail_rows], hit_slot[0], 0, keepdims=False)
    start_tail = jnp.where(hit_mask[0] > 0, start_tail, jnp.zeros((), jnp.bfloat16))
    start_tail = start_tail.reshape(tail_count, channels).astype(f32)
    tail8 = jnp.pad(start_tail, ((8 - tail_count, 0), (0, 0)))
    out_tail = lax.dynamic_index_in_dim(
        rows[:, tail_rows : 2 * tail_rows], inverse[me], 0, keepdims=False
    ).reshape(1, tail_count, channels)

    position = lax.broadcasted_iota(jnp.int32, (steps, 1), 0)
    step = jax.nn.softplus(dt_raw[0] + dt_bias[None, :]) * (position < suffix_len[0]).astype(f32)
    cum = jnp.cumsum(step * (-jnp.exp(a_log))[None, :], axis=0)
    step_b = step.reshape(steps, blocks, HB).transpose(1, 0, 2)
    cum_b = cum.reshape(steps, blocks, HB).transpose(1, 0, 2)
    end_decay = jnp.exp(cum[-1])
    skip_wide = jnp.repeat(d_skip, HEAD_P).reshape(1, heads * HEAD_P)
    bias = conv_bias.reshape(1, channels)

    wide = BLOCKS + 1

    def xs(rows_):
        return pl.BlockSpec((rows_, HBW), lambda g, b: (0, g * wide + b))

    def bcs(rows_):
        return pl.BlockSpec((rows_, HBW), lambda g, b: (0, g * wide + BLOCKS))

    per_block = pl.BlockSpec((1, steps, HB), lambda g, b: (g * BLOCKS + b, 0, 0))
    y_part, c_rows, add = pl.pallas_call(
        scan_kernel,
        grid=(groups_here, BLOCKS),
        in_specs=[
            xs(steps), bcs(steps), xs(8), bcs(8), xs(4), bcs(4), xs(1), bcs(1),
            per_block, per_block,
            pl.BlockSpec((HB, steps), lambda g, b: (g * BLOCKS + b, 0)),
            pl.BlockSpec((1, HBW), lambda g, b: (0, g * BLOCKS + b)),
        ],
        out_specs=[
            pl.BlockSpec((steps, HBW), lambda g, b: (0, g * BLOCKS + b)),
            pl.BlockSpec((steps, NSTATE), lambda g, b: (0, g)),
            pl.BlockSpec((HB, HEAD_P, NSTATE), lambda g, b: (g * BLOCKS + b, 0, 0)),
        ],
        out_shape=[
            jax.ShapeDtypeStruct((steps, heads * HEAD_P), f32),
            jax.ShapeDtypeStruct((steps, groups_here * NSTATE), f32),
            jax.ShapeDtypeStruct((heads, HEAD_P, NSTATE), f32),
        ],
        scratch_shapes=[
            pltpu.VMEM((steps + 8, HBW), f32),
            pltpu.VMEM((steps, NSTATE), f32),
            pltpu.VMEM((steps, steps), f32),
        ],
        compiler_params=pltpu.CompilerParams(vmem_limit_bytes=VMEM),
        cost_estimate=pl.CostEstimate(
            flops=20_000_000_000, bytes_accessed=12_000_000, transcendentals=6_000_000
        ),
    )(
        conv, conv, tail8, tail8, conv_weight, conv_weight, bias, bias,
        step_b, cum_b, cum.T, skip_wide,
    )

    start_state = move_state(slots[0], all_slot, all_mask)

    final = pl.pallas_call(
        final_kernel,
        grid=(blocks,),
        in_specs=[
            pl.BlockSpec(memory_space=pltpu.SMEM),
            pl.BlockSpec((HB, HEAD_P, NSTATE), lambda b: (b, 0, 0)),
            pl.BlockSpec((HB, HEAD_P, NSTATE), lambda b: (b, 0, 0)),
        ],
        out_specs=pl.BlockSpec((HB, HEAD_P, NSTATE), lambda b: (b, 0, 0)),
        out_shape=jax.ShapeDtypeStruct((heads, HEAD_P, NSTATE), jnp.bfloat16),
        compiler_params=pltpu.CompilerParams(vmem_limit_bytes=VMEM),
        cost_estimate=pl.CostEstimate(flops=2_000_000, bytes_accessed=8_000_000, transcendentals=0),
    )(end_decay, add, start_state)

    def prefix(start):
        return pl.pallas_call(
            prefix_kernel,
            grid=(blocks,),
            in_specs=[
                pl.BlockSpec(memory_space=pltpu.SMEM),
                pl.BlockSpec((steps, HBW), lambda b: (0, b)),
                pl.BlockSpec((steps, NSTATE), lambda b: (0, b // BLOCKS)),
                pl.BlockSpec((1, steps, HB), lambda b: (b, 0, 0)),
                pl.BlockSpec((HB, HEAD_P, NSTATE), lambda b: (b, 0, 0)),
            ],
            out_specs=pl.BlockSpec((steps, HBW), lambda b: (0, b)),
            out_shape=jax.ShapeDtypeStruct((steps, heads * HEAD_P), jnp.bfloat16),
            compiler_params=pltpu.CompilerParams(vmem_limit_bytes=VMEM),
            cost_estimate=pl.CostEstimate(
                flops=6_000_000_000, bytes_accessed=9_000_000, transcendentals=100_000
            ),
        )(suffix_len, y_part, c_rows, cum_b, start)

    def two_phase(final, start):
        return move_state(final, inverse, ones), prefix(start)

    def along_line(final, start):
        return relay(final, picks), prefix(start)

    ones = jnp.ones((n,), jnp.int32)
    if n <= LINE:
        picks, most = relay_plan(inverse, ones)
        count = lax.axis_size("groups")
        here = most
        for shift in range(1, count):
            ring = [(i, (i + shift) % count) for i in range(count)]
            most = jnp.maximum(most, lax.ppermute(here, "groups", ring))
        owned, y = lax.cond(most <= 1, along_line, two_phase, final, start_state)
    else:
        owned, y = two_phase(final, start_state)
    return y[None], owned[None], out_tail


def solution(mesh):
    placed = (
        P(("groups", "cache"), None, ("mp", "sub")),
        P(("groups", "cache"), None, ("mp", "sub")),
        P(None, ("mp", "sub")),
        P(("mp", "sub")),
        P(("mp", "sub")),
        P(("mp", "sub")),
        P(("mp", "sub")),
        P(("groups", "cache"), ("mp", "sub"), None, None),
        P(("groups", "cache"), None, ("mp", "sub")),
        P(("groups", "cache")),
        P(("groups", "cache")),
        P(("groups", "cache")),
        P(("groups", "cache")),
    )
    return jax.shard_map(
        per_device,
        mesh=mesh,
        in_specs=placed,
        out_specs=(
            P(("groups", "cache"), None, ("mp", "sub")),
            P(("groups", "cache"), ("mp", "sub"), None, None),
            P(("groups", "cache"), None, ("mp", "sub")),
        ),
        check_vma=False,
    )
```

```python
import functools

import jax
import jax.numpy as jnp
from jax import lax
from jax.experimental import pallas as pl
from jax.experimental.pallas import tpu as pltpu
from jax.sharding import PartitionSpec as P

HEADS = 256
HEAD_P = 64
NSTATE = 256
GROUPS = 8
PER_GROUP = HEADS // GROUPS
HB = 8
HBW = HB * HEAD_P
BLOCKS = PER_GROUP // HB
VMEM = 56 * 1024 * 1024

highest = lax.Precision.HIGHEST
f32 = jnp.float32
MESH = pl.DeviceIdType.MESH
LINE = 4
CHUNKS = 16


def dot(a, b, dims):
    return lax.dot_general(a, b, (dims, ((), ())), precision=highest, preferred_element_type=f32)


def dot_narrow(a, b, dims):
    high = a.astype(jnp.bfloat16)
    low = (a - high.astype(f32)).astype(jnp.bfloat16)
    one = functools.partial(lax.dot_general, dimension_numbers=(dims, ((), ())),
                            preferred_element_type=f32)
    return one(high, b) + one(low, b)


def conv_silu(scratch, x_ref, tail_ref, w_ref, b_ref):
    steps = x_ref.shape[0]
    scratch[0:8, :] = tail_ref[...]
    scratch[8 : 8 + steps, :] = x_ref[...].astype(f32)
    total = b_ref[...]
    for k in range(4):
        total = total + w_ref[k : k + 1, :] * scratch[5 + k : 5 + k + steps, :]
    return total / (1.0 + jnp.exp(-total))


def widen(cols):
    head = lax.broadcasted_iota(jnp.int32, (HB, HBW), 0)
    lane = lax.broadcasted_iota(jnp.int32, (HB, HBW), 1)
    spread = jnp.where(lane // HEAD_P == head, 1.0, 0.0).astype(jnp.bfloat16)
    return dot_narrow(cols, spread, ((1,), (0,)))


def scan_kernel(
    x_ref, bc_ref, tailx_ref, tailbc_ref, wx_ref, wbc_ref, bx_ref, bbc_ref,
    step_ref, cum_ref, cumt_ref, skip_ref,
    y_ref, c_ref, add_ref,
    scratch, b_s, cb_s,
):
    steps = x_ref.shape[0]

    @pl.when(pl.program_id(1) == 0)
    def _():
        bc = conv_silu(scratch, bc_ref, tailbc_ref, wbc_ref, bbc_ref)
        b_s[...] = bc[:, :NSTATE]
        c_ref[...] = bc[:, NSTATE:]
        cb = dot(bc[:, NSTATE:], bc[:, :NSTATE], ((1,), (1,)))
        row = lax.broadcasted_iota(jnp.int32, (steps, steps), 0)
        col = lax.broadcasted_iota(jnp.int32, (steps, steps), 1)
        cb_s[...] = jnp.where(row >= col, cb, 0.0)

    x = conv_silu(scratch, x_ref, tailx_ref, wx_ref, bx_ref)
    cum = cum_ref[0]
    x_scaled = x * widen(step_ref[0])
    x_tail = x_scaled * widen(jnp.exp(cum[steps - 1 : steps, :] - cum))
    add = dot(x_tail, b_s[...], ((0,), (0,)))
    add_ref[...] = add.reshape(HB, HEAD_P, NSTATE)
    lane = lax.broadcasted_iota(jnp.int32, (steps, 2 * HEAD_P), 1)
    for pair in range(HB // 2):
        lo, hi = pair * 2 * HEAD_P, (pair + 1) * 2 * HEAD_P
        both = x_scaled[:, lo:hi]
        parts = []
        for k in (2 * pair, 2 * pair + 1):
            gap = jnp.minimum(cum[:, k : k + 1] - cumt_ref[k : k + 1, :], 0.0)
            parts.append(dot(jnp.exp(gap) * cb_s[...], both, ((1,), (0,))))
        inner = jnp.where(lane < HEAD_P, parts[0], parts[1])
        y_ref[:, lo:hi] = inner + skip_ref[:, lo:hi] * x[:, lo:hi]


def prefix_kernel(len_ref, y_ref, c_ref, cum_ref, state_ref, out_ref):
    steps = y_ref.shape[0]
    state = state_ref[...].reshape(HBW, NSTATE)
    carried = dot_narrow(c_ref[...], state, ((1,), (1,)))
    total = y_ref[...] + carried * widen(jnp.exp(cum_ref[0]))
    row = lax.broadcasted_iota(jnp.int32, (steps, HBW), 0)
    out_ref[...] = jnp.where(row < len_ref[0], total, 0.0).astype(jnp.bfloat16)


def final_kernel(decay_ref, add_ref, state_ref, out_ref):
    base = pl.program_id(0) * HB
    for k in range(HB):
        out_ref[k] = (
            decay_ref[base + k] * state_ref[k].astype(f32) + add_ref[k]
        ).astype(jnp.bfloat16)


def choose_kernel(slot_ref, mask_ref, in_ref, out_ref):
    keep = mask_ref[pl.program_id(0)] > 0
    out_ref[...] = jnp.where(keep, in_ref[...], jnp.zeros_like(in_ref))


def choose(parts, slot, mask):
    count = parts.shape[0]
    block = (1,) + parts.shape[1:]
    return pl.pallas_call(
        choose_kernel,
        grid_spec=pltpu.PrefetchScalarGridSpec(
            num_scalar_prefetch=2,
            grid=(count,),
            in_specs=[pl.BlockSpec(block, lambda r, s, m: (s[r], 0, 0, 0))],
            out_specs=pl.BlockSpec(block, lambda r, s, m: (r, 0, 0, 0)),
        ),
        out_shape=jax.ShapeDtypeStruct(parts.shape, parts.dtype),
        compiler_params=pltpu.CompilerParams(vmem_limit_bytes=VMEM),
        cost_estimate=pl.CostEstimate(flops=0, bytes_accessed=4 * parts.size, transcendentals=0),
    )(slot, mask, parts)


def move_state(state, slot, mask):
    n = lax.axis_size("cache")
    pieces = state.reshape(n, state.shape[0] // n, HEAD_P, NSTATE)
    parts = lax.all_to_all(pieces, "cache", split_axis=0, concat_axis=0, tiled=True)
    chosen = choose(parts, slot, mask)
    return lax.all_to_all(chosen, "cache", split_axis=0, concat_axis=0, tiled=True).reshape(
        state.shape
    )


def relay_kernel(
    n, chunks, pick_ref, own_ref, out_ref,
    right_in, left_in, right_out, left_out, send_r, recv_r, send_l, recv_l,
):
    me = lax.axis_index("cache")
    per = own_ref.shape[0] // chunks
    first, last = me == 0, me == n - 1
    barrier = pltpu.get_barrier_semaphore()

    @pl.when(jnp.logical_not(first))
    def _():
        pl.semaphore_signal(barrier, inc=1, device_id={"cache": me - 1}, device_id_type=MESH)

    @pl.when(jnp.logical_not(last))
    def _():
        pl.semaphore_signal(barrier, inc=1, device_id={"cache": me + 1}, device_id_type=MESH)

    @pl.when(jnp.logical_or(first, last))
    def _():
        pl.semaphore_wait(barrier, 1)

    @pl.when(jnp.logical_not(jnp.logical_or(first, last)))
    def _():
        pl.semaphore_wait(barrier, 2)

    def go_right(c, src):
        return pltpu.make_async_remote_copy(
            src_ref=src.at[pl.ds(c * per, per)], dst_ref=right_in.at[pl.ds(c * per, per)],
            send_sem=send_r.at[c], recv_sem=recv_r.at[c],
            device_id={"cache": lax.rem(me + 1, n)}, device_id_type=MESH,
        )

    def go_left(c, src):
        return pltpu.make_async_remote_copy(
            src_ref=src.at[pl.ds(c * per, per)], dst_ref=left_in.at[pl.ds(c * per, per)],
            send_sem=send_l.at[c], recv_sem=recv_l.at[c],
            device_id={"cache": lax.rem(me + n - 1, n)}, device_id_type=MESH,
        )

    @pl.when(first)
    def _():
        @pl.loop(0, chunks)
        def _(c):
            go_right(c, own_ref).start()

    @pl.when(last)
    def _():
        @pl.loop(0, chunks)
        def _(c):
            go_left(c, own_ref).start()

    @pl.loop(0, chunks + n - 1)
    def _(s):
        cr = s - me
        cl = s - (n - 1 - me)

        @pl.when(jnp.logical_and(jnp.logical_not(first), jnp.logical_and(cr >= 0, cr < chunks)))
        def _():
            go_right(cr, own_ref).wait_recv()

            @pl.when(jnp.logical_not(last))
            def _():
                at = pl.ds(cr * per, per)
                right_out[at] = jnp.where(pick_ref[0] > 0, own_ref[at], right_in[at])
                go_right(cr, right_out).start()

        @pl.when(jnp.logical_and(jnp.logical_not(last), jnp.logical_and(cl >= 0, cl < chunks)))
        def _():
            go_left(cl, own_ref).wait_recv()

            @pl.when(jnp.logical_not(first))
            def _():
                at = pl.ds(cl * per, per)
                left_out[at] = jnp.where(pick_ref[1] > 0, own_ref[at], left_in[at])
                go_left(cl, left_out).start()

    def result(low, high):
        @pl.loop(0, chunks)
        def _(c):
            at = pl.ds(c * per, per)
            value = own_ref[at]
            if low:
                value = jnp.where(pick_ref[2] > 0, right_in[at], value)
            if high:
                value = jnp.where(pick_ref[3] > 0, left_in[at], value)
            out_ref[at] = jnp.where(pick_ref[4] > 0, value, jnp.zeros_like(value))

    @pl.when(first)
    def _():
        result(False, True)

    @pl.when(last)
    def _():
        result(True, False)

    @pl.when(jnp.logical_not(jnp.logical_or(first, last)))
    def _():
        result(True, True)

    @pl.when(jnp.logical_not(last))
    def _():
        @pl.loop(0, chunks)
        def _(c):
            go_right(c, own_ref).wait_send()

    @pl.when(jnp.logical_not(first))
    def _():
        @pl.loop(0, chunks)
        def _(c):
            go_left(c, own_ref).wait_send()


def relay(state, picks):
    n = lax.axis_size("cache")
    chunks = min(CHUNKS, state.shape[0])
    vmem = pl.BlockSpec(memory_space=pltpu.VMEM)
    return pl.pallas_call(
        functools.partial(relay_kernel, n, chunks),
        in_specs=[pl.BlockSpec(memory_space=pltpu.SMEM), vmem],
        out_specs=vmem,
        out_shape=jax.ShapeDtypeStruct(state.shape, state.dtype),
        scratch_shapes=[pltpu.VMEM(state.shape, state.dtype)] * 4
        + [pltpu.SemaphoreType.DMA((chunks,))] * 4,
        compiler_params=pltpu.CompilerParams(
            collective_id=0, has_side_effects=True, vmem_limit_bytes=32 * 1024 * 1024
        ),
        cost_estimate=pl.CostEstimate(
            flops=0, bytes_accessed=100_000_000, transcendentals=0
        ),
    )(picks, state)


def relay_plan(slot, mask):
    n = lax.axis_size("cache")
    me = lax.axis_index("cache")
    ids = jnp.arange(n, dtype=jnp.int32)
    wants = (slot[None, :] == ids[:, None]) & (mask[None, :] > 0)
    right_of = ids[None, :] > ids[:, None]
    right = jnp.any(wants[:, None, :] & right_of[None], axis=2) & (ids[:, None] <= ids[None, :])
    left = jnp.any(wants[:, None, :] & right_of.T[None], axis=2) & (ids[:, None] >= ids[None, :])
    most = jnp.maximum(
        jnp.max(jnp.sum(right.astype(jnp.int32), axis=0)),
        jnp.max(jnp.sum(left.astype(jnp.int32), axis=0)),
    )
    mine = slot[me]
    picks = jnp.stack([right[me, me], left[me, me], mine < me, mine > me, mask[me] > 0])
    return picks.astype(jnp.int32), most


def per_device(
    conv_input, dt_raw, conv_weight, conv_bias, dt_bias, a_log, d_skip,
    cache_state, cache_tail, hit_slot, hit_mask, suffix_len, write_slot,
):
    conv = conv_input[0]
    steps, channels = conv.shape
    heads = dt_raw.shape[2]
    tail_count = cache_tail.shape[1]
    groups_here = heads // PER_GROUP
    blocks = groups_here * BLOCKS
    n = lax.axis_size("cache")
    me = lax.axis_index("cache")

    new_tail = lax.dynamic_slice_in_dim(conv, suffix_len[0] - tail_count, tail_count, 0)
    ints = jnp.concatenate([hit_slot, hit_mask, write_slot]).astype(jnp.bfloat16)
    row = jnp.concatenate(
        [
            cache_tail.reshape(-1, 128),
            new_tail.reshape(-1, 128),
            jnp.pad(ints, (0, 125)).reshape(1, 128),
        ],
        axis=0,
    )
    if n <= LINE:
        steps_by = [row] + [
            lax.ppermute(row, "cache", [(i, (i + shift) % n) for i in range(n)])
            for shift in range(1, n)
        ]
        came = jnp.stack(steps_by)
        rows = jnp.stack(
            [lax.dynamic_index_in_dim(came, (me - i) % n, 0, keepdims=False) for i in range(n)]
        )
    else:
        rows = lax.all_to_all(
            jnp.broadcast_to(row[None], (n,) + row.shape), "cache", split_axis=0, concat_axis=0,
            tiled=True,
        )
    table = rows[:, -1, :3].astype(jnp.int32)
    all_slot, all_mask, all_write = table[:, 0], table[:, 1], table[:, 2]
    ids = jnp.arange(n, dtype=jnp.int32)
    inverse = jnp.sum(jnp.where(all_write[None, :] == ids[:, None], ids[None, :], 0), axis=1)
    tail_rows = tail_count * channels // 128
    start_tail = lax.dynamic_index_in_dim(rows[:, :tail_rows], hit_slot[0], 0, keepdims=False)
    start_tail = jnp.where(hit_mask[0] > 0, start_tail, jnp.zeros((), jnp.bfloat16))
    start_tail = start_tail.reshape(tail_count, channels).astype(f32)
    tail8 = jnp.pad(start_tail, ((8 - tail_count, 0), (0, 0)))
    out_tail = lax.dynamic_index_in_dim(
        rows[:, tail_rows : 2 * tail_rows], inverse[me], 0, keepdims=False
    ).reshape(1, tail_count, channels)

    position = lax.broadcasted_iota(jnp.int32, (steps, 1), 0)
    step = jax.nn.softplus(dt_raw[0] + dt_bias[None, :]) * (position < suffix_len[0]).astype(f32)
    cum = jnp.cumsum(step * (-jnp.exp(a_log))[None, :], axis=0)
    step_b = step.reshape(steps, blocks, HB).transpose(1, 0, 2)
    cum_b = cum.reshape(steps, blocks, HB).transpose(1, 0, 2)
    end_decay = jnp.exp(cum[-1])
    skip_wide = jnp.repeat(d_skip, HEAD_P).reshape(1, heads * HEAD_P)
    bias = conv_bias.reshape(1, channels)

    wide = BLOCKS + 1

    def xs(rows_):
        return pl.BlockSpec((rows_, HBW), lambda g, b: (0, g * wide + b))

    def bcs(rows_):
        return pl.BlockSpec((rows_, HBW), lambda g, b: (0, g * wide + BLOCKS))

    per_block = pl.BlockSpec((1, steps, HB), lambda g, b: (g * BLOCKS + b, 0, 0))
    y_part, c_rows, add = pl.pallas_call(
        scan_kernel,
        grid=(groups_here, BLOCKS),
        in_specs=[
            xs(steps), bcs(steps), xs(8), bcs(8), xs(4), bcs(4), xs(1), bcs(1),
            per_block, per_block,
            pl.BlockSpec((HB, steps), lambda g, b: (g * BLOCKS + b, 0)),
            pl.BlockSpec((1, HBW), lambda g, b: (0, g * BLOCKS + b)),
        ],
        out_specs=[
            pl.BlockSpec((steps, HBW), lambda g, b: (0, g * BLOCKS + b)),
            pl.BlockSpec((steps, NSTATE), lambda g, b: (0, g)),
            pl.BlockSpec((HB, HEAD_P, NSTATE), lambda g, b: (g * BLOCKS + b, 0, 0)),
        ],
        out_shape=[
            jax.ShapeDtypeStruct((steps, heads * HEAD_P), f32),
            jax.ShapeDtypeStruct((steps, groups_here * NSTATE), f32),
            jax.ShapeDtypeStruct((heads, HEAD_P, NSTATE), f32),
        ],
        scratch_shapes=[
            pltpu.VMEM((steps + 8, HBW), f32),
            pltpu.VMEM((steps, NSTATE), f32),
            pltpu.VMEM((steps, steps), f32),
        ],
        compiler_params=pltpu.CompilerParams(vmem_limit_bytes=VMEM),
        cost_estimate=pl.CostEstimate(
            flops=20_000_000_000, bytes_accessed=12_000_000, transcendentals=6_000_000
        ),
    )(
        conv, conv, tail8, tail8, conv_weight, conv_weight, bias, bias,
        step_b, cum_b, cum.T, skip_wide,
    )

    start_state = move_state(cache_state[0], all_slot, all_mask)

    final = pl.pallas_call(
        final_kernel,
        grid=(blocks,),
        in_specs=[
            pl.BlockSpec(memory_space=pltpu.SMEM),
            pl.BlockSpec((HB, HEAD_P, NSTATE), lambda b: (b, 0, 0)),
            pl.BlockSpec((HB, HEAD_P, NSTATE), lambda b: (b, 0, 0)),
        ],
        out_specs=pl.BlockSpec((HB, HEAD_P, NSTATE), lambda b: (b, 0, 0)),
        out_shape=jax.ShapeDtypeStruct((heads, HEAD_P, NSTATE), jnp.bfloat16),
        compiler_params=pltpu.CompilerParams(vmem_limit_bytes=VMEM),
        cost_estimate=pl.CostEstimate(flops=2_000_000, bytes_accessed=8_000_000, transcendentals=0),
    )(end_decay, add, start_state)

    def prefix(start):
        return pl.pallas_call(
            prefix_kernel,
            grid=(blocks,),
            in_specs=[
                pl.BlockSpec(memory_space=pltpu.SMEM),
                pl.BlockSpec((steps, HBW), lambda b: (0, b)),
                pl.BlockSpec((steps, NSTATE), lambda b: (0, b // BLOCKS)),
                pl.BlockSpec((1, steps, HB), lambda b: (b, 0, 0)),
                pl.BlockSpec((HB, HEAD_P, NSTATE), lambda b: (b, 0, 0)),
            ],
            out_specs=pl.BlockSpec((steps, HBW), lambda b: (0, b)),
            out_shape=jax.ShapeDtypeStruct((steps, heads * HEAD_P), jnp.bfloat16),
            compiler_params=pltpu.CompilerParams(vmem_limit_bytes=VMEM),
            cost_estimate=pl.CostEstimate(
                flops=6_000_000_000, bytes_accessed=9_000_000, transcendentals=100_000
            ),
        )(suffix_len, y_part, c_rows, cum_b, start)

    def two_phase(final, start):
        return move_state(final, inverse, ones), prefix(start)

    def along_line(final, start):
        return relay(final, picks), prefix(start)

    ones = jnp.ones((n,), jnp.int32)
    if n <= LINE:
        picks, most = relay_plan(inverse, ones)
        count = lax.axis_size("groups")
        here = most
        for shift in range(1, count):
            ring = [(i, (i + shift) % count) for i in range(count)]
            most = jnp.maximum(most, lax.ppermute(here, "groups", ring))
        owned, y = lax.cond(most <= 1, along_line, two_phase, final, start_state)
    else:
        owned, y = two_phase(final, start_state)
    return y[None], owned[None], out_tail


def solution(mesh):
    placed = (
        P(("groups", "cache"), None, ("mp", "sub")),
        P(("groups", "cache"), None, ("mp", "sub")),
        P(None, ("mp", "sub")),
        P(("mp", "sub")),
        P(("mp", "sub")),
        P(("mp", "sub")),
        P(("mp", "sub")),
        P(("groups", "cache"), ("mp", "sub"), None, None),
        P(("groups", "cache"), None, ("mp", "sub")),
        P(("groups", "cache")),
        P(("groups", "cache")),
        P(("groups", "cache")),
        P(("groups", "cache")),
    )
    return jax.shard_map(
        per_device,
        mesh=mesh,
        in_specs=placed,
        out_specs=(
            P(("groups", "cache"), None, ("mp", "sub")),
            P(("groups", "cache"), ("mp", "sub"), None, None),
            P(("groups", "cache"), None, ("mp", "sub")),
        ),
        check_vma=False,
    )
```
